256 devices in a mesh: row: 16 (over z, x_hi), col: 16 (over x_lo, y, core).
Axes of the slice: x: 4 (x_hi: 2, x_lo: 2; x = x_hi * 2 + x_lo), y: 4, z: 8, core: 2. Of those that a mesh axis runs over, the one named last changes fastest.
Arguments:
- inverse: float32 [24576, 24576], P('row', 'col'), may hold values from -0.15625 to 0.15625
- pattern: int32 [48, 48], replicated, may hold values from 0 to 1, as said below
- factor: float32 [24576, 1024], P(('row', 'col')), may hold values from -0.3125 to 0.3125
- diag_inverse: float32 [1024, 1024], replicated, may hold values from -6 to 6
Outputs:
- panel_out: float32 [24576, 1024], P(('row', 'col'))
- diag_block: float32 [1024, 1024], replicated
The draws below stay inside these ranges and needn't reach their ends.
Inputs may be any that keep to these rules, and one draw needn't show every extreme that they name: pattern[i, j] is 1 where tile (i, j) of the inverse is stored, else 0.
All inputs are finite; a program needn't handle non-finite values.
Results may differ from the reference program's by a relative error of at most 0.000075.
Values sent between devices are 32-bit elements; how exact they have to be, the bound alone decides.
A program may use at most 128 MiB of HBM per device.

```python
import jax
import jax.numpy as jnp
from jax import lax

B = 512
W = 1024
TILES = 48
ANC = 24576
N_ROW = 16
N_COL = 16


def draw_pattern(key, part):
    level_key = jax.random.fold_in(key, 11)
    roll_key = jax.random.fold_in(key, 12)
    exponent = jax.random.randint(level_key, (N_ROW, N_COL), 0, 4)
    levels = jnp.power(2, exponent).astype(jnp.int32)
    spread_levels = jnp.repeat(jnp.repeat(levels, TILES // N_ROW, 0), TILES // N_COL, 1)
    rolls = jax.random.randint(roll_key, (TILES, TILES), 0, 8)
    return (rolls < spread_levels).astype(jnp.int32)


def block_levels(key, shape, cuts, low, high):
    level = 1.0
    for position, parts in cuts:
        draws = jax.random.uniform(jax.random.fold_in(jax.random.fold_in(key, 6), position), (parts,), jnp.float32, low / len(cuts), high / len(cuts))
        level = level * jnp.repeat(jnp.exp(draws), shape[position] // parts).reshape((-1,) + (1,) * (len(shape) - 1 - position))
    return level


def bell_draw(stream_key, dims, width, most, split=(), kind=jnp.bfloat16):
    values = width * jax.random.normal(stream_key, dims, jnp.float32)
    if split:
        values = values * block_levels(stream_key, dims, split, -0.22, 0.18)
    return jnp.clip(values, -most, most).astype(kind)


def setup_inputs(seed: int = 0) -> dict:
    splits = jax.random.split(jax.random.key(seed), 5)
    inverse = bell_draw(splits[0], (ANC, ANC), (ANC // 16) ** -0.5, 0.15625, ((0, 16), (1, 16)), jnp.float32)
    pattern = draw_pattern(jax.random.fold_in(splits[4], 71), 0)
    factor = bell_draw(splits[2], (ANC, W), (ANC // 64) ** -0.5, 0.3125, ((0, 256),), jnp.float32)
    diag_inverse = bell_draw(splits[3], (W, W), 1.0, 6.0, (), jnp.float32)
    return {"inverse": inverse, "pattern": pattern, "factor": factor, "diag_inverse": diag_inverse}


HIGHEST = lax.Precision.HIGHEST


def reference(inverse, pattern, factor, diag_inverse):
    def strip_product(tile_index):
        row_strip = lax.dynamic_slice_in_dim(inverse, tile_index * B, B, 0)
        keep_mask = jnp.repeat(pattern[tile_index], B).astype(row_strip.dtype)
        return jnp.dot(row_strip * keep_mask[None, :], factor, precision=HIGHEST)

    products = lax.map(strip_product, jnp.arange(TILES, dtype=jnp.int32))
    panel_out = -products.reshape(ANC, W)
    diag_block = diag_inverse - jnp.dot(factor.T, panel_out, precision=HIGHEST)
    return panel_out, diag_block
```

```python
import functools

import jax
import jax.numpy as jnp
from jax import lax
from jax.experimental import pallas as pl
from jax.experimental.pallas import tpu as pltpu
from jax.sharding import PartitionSpec as P

MESH = pl.DeviceIdType.MESH
F32 = jnp.float32
BF16 = jnp.bfloat16

FULL = {"NZ": 8, "XH": 2, "XL": 2, "NY": 4, "W": 1024, "CH": 256, "RB": 96, "B": 512}
STAGES = {"rx": 8, "ry": 11, "dot": 13, "dy": 15, "dx": 17, "dz": 19, "az": 22, "ax": 24, "ay": 26, "ac": 27, "out": 28}


def split(value):
    high = value.astype(BF16)
    return high, (value - high.astype(F32)).astype(BF16)


def kernel(
    g, inv_hbm, pat_ref, fac_ref, dinv_hbm, panel_ref, diag_hbm,
    stage, ih, il, gath, fh, fl, part, rc, rx, ry, fth, ftl, dpart, dc, dy, dx, dz, full, dinv,
    load_sem, got, src_sem, fwd_sem, rc_s, rc_r, rx_s, rx_r, ry_s, ry_r, dc_s, dc_r, dy_s, dy_r, dx_s, dx_r,
    dz_s, dz_r, az_s, az_r, ax_s, ax_r, ay_s, ay_r, ac_s, ac_r, out_sem,
):
    nz, xhn, xln, ny, w, ch, rb = (g[k] for k in ("NZ", "XH", "XL", "NY", "W", "CH", "RB"))
    nx, chunks, ncol = xhn * xln, w // ch, xln * ny * 2
    half = rb // 2
    row, col = lax.axis_index("row"), lax.axis_index("col")
    z, xh = row // xhn, row % xhn
    core, y, xl = col % 2, (col // 2) % ny, col // (2 * ny)
    x = xh * xln + xl

    def at(z_, x_, y_, core_):
        return (z_ * xhn + x_ // xln, (x_ % xln) * (2 * ny) + y_ * 2 + core_)

    def z_peer(j):
        return at(lax.rem(z + j, nz), x, y, core)

    def x_peer(j):
        return at(z, lax.rem(x + j, nx), y, core)

    def y_peer(j):
        return at(z, x, lax.rem(y + j, ny), core)

    sibling = at(z, x, y, 1 - core)
    x_next = at(z, xh * xln + (xln - 1 - xl), y, core)
    z_root = col // 2
    up = lax.rem(z - z_root + nz, nz)
    down = lax.rem(nz - up, nz)
    is_root = up == 0
    on_diag = row == col

    def remote(src, dst, send, recv, dev):
        return pltpu.make_async_remote_copy(
            src_ref=src, dst_ref=dst, send_sem=send, recv_sem=recv, device_id=dev, device_id_type=MESH
        )

    def landed(ref, recv):
        remote(ref, ref, recv, recv, sibling).wait_recv()

    def sent(ref, send):
        remote(ref, ref, send, send, sibling).wait_send()

    load = pltpu.make_async_copy(inv_hbm, stage, load_sem.at[0])
    load.start()
    d_half, d_y, d_x = w // 2, w // 2 // ny, w // 2 // ny // nx
    lanes = ch // 128
    d_z = d_x * lanes // nz
    y_base = core * d_half + y * d_y
    x_base = y_base + x * d_x

    def z_place(z_):
        first = pl.multiple_of(x_base + (z_ // lanes) * d_z, d_z)
        return pl.ds(first, d_z), pl.ds(pl.multiple_of((z_ % lanes) * 128, 128), 128)

    def rows_of(first, size):
        return pl.ds(pl.multiple_of(first, size), size)

    z_rows, z_lanes = z_place(z)

    def dinv_copy(k):
        first = pl.multiple_of(k * ch + (z % lanes) * 128, 128)
        return pltpu.make_async_copy(dinv_hbm.at[z_rows, pl.ds(first, 128)], dinv.at[k], load_sem.at[1 + k])

    for k in range(chunks):
        dinv_copy(k).start()

    barrier = pltpu.get_barrier_semaphore()

    def greet(dev):
        pl.semaphore_signal(barrier, inc=1, device_id=dev, device_id_type=MESH)

    greet(sibling)
    for j in range(1, nz):
        greet(z_peer(j))
    for j in range(1, nx):
        greet(x_peer(j))
    for j in range(1, ny):
        greet(y_peer(j))
    others = 1 + (nz - 1) + (nx - 1) + (ny - 1)
    for a in range(xhn):
        pl.when(jnp.logical_not(jnp.logical_and(on_diag, xh == a)))(lambda a=a: greet((z * xhn + a, row)))

    @pl.when(is_root)
    def _():
        @pl.loop(0, ncol)
        def _(j):
            pl.when(jnp.logical_not(jnp.logical_and(on_diag, j == col)))(lambda: greet((z * xhn + core, j)))

    mine = jnp.where(on_diag, 1, 0)
    pl.semaphore_wait(barrier, others + xhn - mine + jnp.where(is_root, ncol - mine, 0))

    def send_source(k):
        for a in range(xhn):
            here = jnp.logical_and(on_diag, xh == a)
            for way in range(2):
                src = fac_ref.at[pl.ds(way * half, half), pl.ds(pl.multiple_of(k * ch, ch), ch)]
                dst = gath.at[way, k, col]

                @pl.when(jnp.logical_not(here))
                def _(src=src, dst=dst, way=way, a=a):
                    remote(src, dst, src_sem, got.at[way, k, col], (z * xhn + a, row)).start()

                @pl.when(here)
                def _(src=src, dst=dst, way=way):
                    pltpu.make_async_copy(src, dst, got.at[way, k, col]).start()

    for k in range(min(2, chunks)):
        send_source(k)
    turned = fac_ref[...].T
    fth[...], ftl[...] = split(turned)
    load.wait()

    def mask_rows(i):
        block, part_of = i // (rb // 32), i % (rb // 32)
        dest = rows_of(((block % 2) * (ncol // 2) + block // 2) * rb + part_of * 32, 32)
        tiles = (rb * ncol) // g["B"]
        tile_row = (i * 32) // g["B"]
        for j in range(tiles):
            keep = pat_ref[row * tiles + tile_row, col * tiles + j].astype(F32)
            cols = pl.ds(j * g["B"], g["B"])
            ih[dest, cols], il[dest, cols] = split(stage[rows_of(i * 32, 32), cols] * keep)

    per = ncol // 4

    def gather_step(k, h):
        @pl.loop(0, per)
        def _(n):
            i = h * per + n
            for way, far, step in ((0, up, 1), (1, down, nz - 1)):
                piece = gath.at[way, k, i]
                landed(piece, got.at[way, k, i])
                pl.when(far < nz - 1)(
                    lambda piece=piece, way=way, step=step: remote(
                        piece, piece, fwd_sem.at[way], got.at[way, k, i], z_peer(step)
                    ).start()
                )
                rows = rows_of(i * rb + way * half, half)
                fh[k, rows, :], fl[k, rows, :] = split(gath[way, k, i])

    m = rb * ncol // 4
    mine_rows = rb * ncol // 2

    def product(k, h):
        rows = rows_of(h * m, m)
        left_h, left_l = ih[rows, :], il[rows, :]
        right_h, right_l = fh[k], fl[k]
        total = jnp.dot(left_h, right_h, preferred_element_type=F32)
        total += jnp.dot(left_h, right_l, preferred_element_type=F32)
        total += jnp.dot(left_l, right_h, preferred_element_type=F32)
        part[k, rows, :] = total

    def rc_send(k):
        remote(part.at[k, rows_of((1 - core) * mine_rows, mine_rows)], rc.at[k], rc_s, rc_r.at[k], sibling).start()

    core_base = core * mine_rows
    x_rows = mine_rows // xln

    def rx_stage(k):
        landed(rc.at[k], rc_r.at[k])
        own = rows_of(core_base, mine_rows)
        part[k, own, :] += rc[k]
        if xln > 1:
            remote(part.at[k, rows_of(core_base + (1 - xl) * x_rows, x_rows)], rx.at[k], rx_s, rx_r.at[k], x_next).start()

    def ry_stage(k):
        base = core_base + xl * x_rows
        if xln > 1:
            landed(rx.at[k], rx_r.at[k])
            own = rows_of(base, x_rows)
            part[k, own, :] += rx[k]
        for j in range(1, ny):
            rows = rows_of(base + lax.rem(y + j, ny) * rb, rb)
            remote(part.at[k, rows], ry.at[k, j - 1], ry_s, ry_r.at[k], y_peer(j)).start()

    def dot_stage(k):
        landed(ry.at[k], ry_r.at[k])
        total = part[k, rows_of(core_base + xl * x_rows + y * rb, rb), :]
        for j in range(ny - 1):
            total += ry[k, j]
        panel_ref[k] = -total
        right_h, right_l = split(total)
        update = jnp.dot(fth[...], right_h, preferred_element_type=F32)
        update += jnp.dot(fth[...], right_l, preferred_element_type=F32)
        update += jnp.dot(ftl[...], right_h, preferred_element_type=F32)
        dpart[k] = update
        remote(dpart.at[k, rows_of((1 - core) * d_half, d_half)], dc.at[k], dc_s, dc_r.at[k], sibling).start()

    def dy_stage(k):
        landed(dc.at[k], dc_r.at[k])
        dpart[k, rows_of(core * d_half, d_half), :] += dc[k]
        for j in range(1, ny):
            rows = rows_of(core * d_half + lax.rem(y + j, ny) * d_y, d_y)
            remote(dpart.at[k, rows], dy.at[k, j - 1], dy_s, dy_r.at[k], y_peer(j)).start()

    def dx_stage(k):
        landed(dy.at[k], dy_r.at[k])
        own = rows_of(y_base, d_y)
        dpart[k, own, :] += functools.reduce(lambda a, b: a + b, [dy[k, j] for j in range(ny - 1)])
        for j in range(1, nx):
            rows = rows_of(y_base + lax.rem(x + j, nx) * d_x, d_x)
            remote(dpart.at[k, rows], dx.at[k, j - 1], dx_s, dx_r.at[k], x_peer(j)).start()

    def dz_stage(k):
        landed(dx.at[k], dx_r.at[k])
        own = rows_of(x_base, d_x)
        dpart[k, own, :] += functools.reduce(lambda a, b: a + b, [dx[k, j] for j in range(nx - 1)])
        for j in range(1, nz):
            rows, cols = z_place(lax.rem(z + j, nz))
            remote(dpart.at[k, rows, cols], dz.at[k, j - 1], dz_s, dz_r.at[k], z_peer(j)).start()

    def az_stage(k):
        landed(dz.at[k], dz_r.at[k])
        total = dpart[k, z_rows, z_lanes] + dinv[k]
        for j in range(nz - 1):
            total += dz[k, j]
        full[k, z_rows, z_lanes] = total
        place = full.at[k, z_rows, z_lanes]
        for j in range(1, nz):
            remote(place, place, az_s, az_r.at[k], z_peer(j)).start()

    def ax_stage(k):
        landed(dz.at[k], az_r.at[k])
        place = full.at[k, rows_of(x_base, d_x)]
        for j in range(1, nx):
            remote(place, place, ax_s, ax_r.at[k], x_peer(j)).start()

    def ay_stage(k):
        landed(dx.at[k], ax_r.at[k])
        place = full.at[k, rows_of(y_base, d_y)]
        for j in range(1, ny):
            remote(place, place, ay_s, ay_r.at[k], y_peer(j)).start()

    def ac_stage(k):
        landed(dy.at[k], ay_r.at[k])
        place = full.at[k, rows_of(core * d_half, d_half)]
        remote(place, place, ac_s, ac_r.at[k], sibling).start()

    def out_copy(k):
        cols = pl.ds(pl.multiple_of(k * ch, ch), ch)
        return pltpu.make_async_copy(full.at[k], diag_hbm.at[:, cols], out_sem.at[k])

    def out_stage(k):
        landed(dc.at[k], ac_r.at[k])
        out_copy(k).start()

    for k in range(chunks):
        dinv_copy(k).wait()

    stages = {
        "rx": rx_stage, "ry": ry_stage, "dot": dot_stage, "dy": dy_stage, "dx": dx_stage, "dz": dz_stage,
        "az": az_stage, "ax": ax_stage, "ay": ay_stage, "ac": ac_stage, "out": out_stage,
    }
    masks = rb * ncol // 32 // 4

    @pl.loop(0, 4 * (chunks - 1) + STAGES["out"] + 1)
    def _(u):
        k, h = u // 4, u % 4

        @pl.when(u < 4 * chunks)
        def _():
            pl.when(jnp.logical_and(h == 0, k + 2 < chunks))(lambda: send_source(k + 2))
            gather_step(k, h)

        @pl.when(u < 4)
        def _():
            @pl.loop(0, masks)
            def _(n):
                mask_rows(u * masks + n)

        @pl.when(jnp.logical_and(u >= 4, u < 4 * chunks + 4))
        def _():
            product(k - 1, h)
            pl.when(h == 3)(lambda: rc_send(k - 1))

        for name, after in sorted(STAGES.items(), key=lambda item: -item[1]):
            since = u - after
            runs = jnp.logical_and(h == after % 4, jnp.logical_and(since >= 0, since < 4 * chunks))
            pl.when(runs)(lambda name=name, since=since: stages[name](since // 4))

    for k in range(chunks):
        out_copy(k).wait()
    sent(fac_ref, src_sem)
    pl.when(jnp.logical_not(on_diag))(lambda: sent(fac_ref, src_sem))
    pl.when(up < nz - 1)(lambda: sent(gath.at[0], fwd_sem.at[0]))
    pl.when(down < nz - 1)(lambda: sent(gath.at[1], fwd_sem.at[1]))
    sent(rc, rc_s)
    if xln > 1:
        sent(rx, rx_s)
    for ref, sem in ((ry, ry_s), (dc, dc_s), (dy, dy_s), (dx, dx_s), (dz, dz_s), (dz, az_s), (dx, ax_s), (dy, ay_s), (dc, ac_s)):
        sent(ref, sem)


def make(g):
    nz, xhn, xln, ny, w, ch, rb = (g[k] for k in ("NZ", "XH", "XL", "NY", "W", "CH", "RB"))
    nx, chunks, ncol = xhn * xln, w // ch, xln * ny * 2
    n = rb * ncol
    dma = pltpu.SemaphoreType.DMA
    d_half, d_y, d_x = w // 2, w // 2 // ny, w // 2 // ny // nx
    d_z = d_x * (ch // 128) // nz

    def body(inverse, pattern, factor, diag_inverse):
        panel, diag = pl.pallas_call(
            functools.partial(kernel, g),
            out_shape=(jax.ShapeDtypeStruct((chunks, rb, ch), F32), jax.ShapeDtypeStruct((w, w), F32)),
            in_specs=[
                pl.BlockSpec(memory_space=pl.ANY),
                pl.BlockSpec(memory_space=pltpu.SMEM),
                pl.BlockSpec(memory_space=pltpu.VMEM),
                pl.BlockSpec(memory_space=pl.ANY),
            ],
            out_specs=(pl.BlockSpec(memory_space=pltpu.VMEM), pl.BlockSpec(memory_space=pl.ANY)),
            scratch_shapes=[
                pltpu.VMEM((n, n), F32),
                pltpu.VMEM((n, n), BF16),
                pltpu.VMEM((n, n), BF16),
                pltpu.VMEM((2, chunks, ncol, rb // 2, ch), F32),
                pltpu.VMEM((chunks, n, ch), BF16),
                pltpu.VMEM((chunks, n, ch), BF16),
                pltpu.VMEM((chunks, n, ch), F32),
                pltpu.VMEM((chunks, n // 2, ch), F32),
                pltpu.VMEM((chunks, n // 2 // xln, ch), F32),
                pltpu.VMEM((chunks, ny - 1, rb, ch), F32),
                pltpu.VMEM((w, rb), BF16),
                pltpu.VMEM((w, rb), BF16),
                pltpu.VMEM((chunks, w, ch), F32),
                pltpu.VMEM((chunks, d_half, ch), F32),
                pltpu.VMEM((chunks, ny - 1, d_y, ch), F32),
                pltpu.VMEM((chunks, nx - 1, d_x, ch), F32),
                pltpu.VMEM((chunks, nz - 1, d_z, 128), F32),
                pltpu.VMEM((chunks, w, ch), F32),
                pltpu.VMEM((chunks, d_z, 128), F32),
                dma((1 + chunks,)),
                dma((2, chunks, ncol)),
                dma,
                dma((2,)),
            ]
            + [dma, dma((chunks,))] * 11
            + [dma((chunks,))],
            compiler_params=pltpu.CompilerParams(
                collective_id=0, has_side_effects=True, vmem_limit_bytes=63 * 2**20
            ),
        )(inverse, pattern, factor, diag_inverse)
        return panel.transpose(1, 0, 2).reshape(rb, w), diag

    return body


def solution(mesh):
    return jax.shard_map(
        make(FULL),
        mesh=mesh,
        in_specs=(P("row", "col"), P(), P(("row", "col"), None), P()),
        out_specs=(P(("row", "col"), None), P()),
        check_vma=False,
    )
```

```python
import functools

import jax
import jax.numpy as jnp
from jax import lax
from jax.experimental import pallas as pl
from jax.experimental.pallas import tpu as pltpu
from jax.sharding import PartitionSpec as P

MESH = pl.DeviceIdType.MESH
F32 = jnp.float32
BF16 = jnp.bfloat16

FULL = {"NZ": 8, "XH": 2, "XL": 2, "NY": 4, "W": 1024, "CH": 256, "RB": 96, "B": 512}
STAGES = {'rx': 1, 'ry': 4, 'dot': 7, 'dy': 8, 'dx': 11, 'dz': 13, 'az': 15, 'ax': 17, 'ay': 19, 'ac': 22, 'out': 23}
HOP = 5


def split(value):
    high = value.astype(BF16)
    return high, (value - high.astype(F32)).astype(BF16)


def kernel(
    g, inv_hbm, pat_ref, fac_ref, dinv_hbm, panel_ref, diag_hbm,
    stage, ih, il, gath, fh, fl, part, rc, rx, ry, fth, ftl, dpart, dc, dy, dx, dz, full, dinv,
    load_sem, got, src_sem, fwd_sem, rc_s, rc_r, rx_s, rx_r, ry_s, ry_r, dc_s, dc_r, dy_s, dy_r, dx_s, dx_r,
    dz_s, dz_r, az_s, az_r, ax_s, ax_r, ay_s, ay_r, ac_s, ac_r, out_sem,
):
    nz, xhn, xln, ny, w, ch, rb = (g[k] for k in ("NZ", "XH", "XL", "NY", "W", "CH", "RB"))
    nx, chunks, ncol = xhn * xln, w // ch, xln * ny * 2
    half = rb // 2
    row, col = lax.axis_index("row"), lax.axis_index("col")
    z, xh = row // xhn, row % xhn
    core, y, xl = col % 2, (col // 2) % ny, col // (2 * ny)
    x = xh * xln + xl

    def at(z_, x_, y_, core_):
        return (z_ * xhn + x_ // xln, (x_ % xln) * (2 * ny) + y_ * 2 + core_)

    def z_peer(j):
        return at(lax.rem(z + j, nz), x, y, core)

    def x_peer(j):
        return at(z, lax.rem(x + j, nx), y, core)

    def y_peer(j):
        return at(z, x, lax.rem(y + j, ny), core)

    sibling = at(z, x, y, 1 - core)
    x_next = at(z, xh * xln + (xln - 1 - xl), y, core)
    z_root = col // 2
    up = lax.rem(z - z_root + nz, nz)
    down = lax.rem(nz - up, nz)
    is_root = up == 0
    on_diag = row == col

    def remote(src, dst, send, recv, dev):
        return pltpu.make_async_remote_copy(
            src_ref=src, dst_ref=dst, send_sem=send, recv_sem=recv, device_id=dev, device_id_type=MESH
        )

    def landed(ref, recv):
        remote(ref, ref, recv, recv, sibling).wait_recv()

    def sent(ref, send):
        remote(ref, ref, send, send, sibling).wait_send()

    load = pltpu.make_async_copy(inv_hbm, stage, load_sem.at[0])
    load.start()
    d_half, d_y, d_x = w // 2, w // 2 // ny, w // 2 // ny // nx
    lanes = ch // 128
    d_z = d_x * lanes // nz
    y_base = core * d_half + y * d_y
    x_base = y_base + x * d_x

    def z_place(z_):
        first = pl.multiple_of(x_base + (z_ // lanes) * d_z, d_z)
        return pl.ds(first, d_z), pl.ds(pl.multiple_of((z_ % lanes) * 128, 128), 128)

    def rows_of(first, size):
        return pl.ds(pl.multiple_of(first, size), size)

    z_rows, z_lanes = z_place(z)

    def dinv_copy(k):
        first = pl.multiple_of(k * ch + (z % lanes) * 128, 128)
        return pltpu.make_async_copy(dinv_hbm.at[z_rows, pl.ds(first, 128)], dinv.at[k], load_sem.at[1 + k])

    for k in range(chunks):
        dinv_copy(k).start()

    barrier = pltpu.get_barrier_semaphore()

    def greet(dev):
        pl.semaphore_signal(barrier, inc=1, device_id=dev, device_id_type=MESH)

    greet(sibling)
    for j in range(1, nz):
        greet(z_peer(j))
    for j in range(1, nx):
        greet(x_peer(j))
    for j in range(1, ny):
        greet(y_peer(j))
    others = 1 + (nz - 1) + (nx - 1) + (ny - 1)
    for a in range(xhn):
        pl.when(jnp.logical_not(jnp.logical_and(on_diag, xh == a)))(lambda a=a: greet((z * xhn + a, row)))

    @pl.when(is_root)
    def _():
        @pl.loop(0, ncol)
        def _(j):
            pl.when(jnp.logical_not(jnp.logical_and(on_diag, j == col)))(lambda: greet((z * xhn + core, j)))

    mine = jnp.where(on_diag, 1, 0)
    pl.semaphore_wait(barrier, others + xhn - mine + jnp.where(is_root, ncol - mine, 0))

    def send_source(k):
        for a in range(xhn):
            here = jnp.logical_and(on_diag, xh == a)
            for way in range(2):
                src = fac_ref.at[pl.ds(way * half, half), pl.ds(pl.multiple_of(k * ch, ch), ch)]
                dst = gath.at[way, k, col]

                @pl.when(jnp.logical_not(here))
                def _(src=src, dst=dst, way=way, a=a):
                    remote(src, dst, src_sem, got.at[way, k, col], (z * xhn + a, row)).start()

                @pl.when(here)
                def _(src=src, dst=dst, way=way):
                    pltpu.make_async_copy(src, dst, got.at[way, k, col]).start()

    for k in range(min(2, chunks)):
        send_source(k)
    turned = fac_ref[...].T
    fth[...], ftl[...] = split(turned)
    load.wait()

    def mask_rows(i):
        block, part_of = i // (rb // 32), i % (rb // 32)
        dest = rows_of(((block % 2) * (ncol // 2) + block // 2) * rb + part_of * 32, 32)
        tiles = (rb * ncol) // g["B"]
        tile_row = (i * 32) // g["B"]
        for j in range(tiles):
            keep = pat_ref[row * tiles + tile_row, col * tiles + j].astype(F32)
            cols = pl.ds(j * g["B"], g["B"])
            ih[dest, cols], il[dest, cols] = split(stage[rows_of(i * 32, 32), cols] * keep)

    per = ncol // 4

    pieces = chunks * ncol

    def gather_step(t):
        for way, far, step in ((0, up, 1), (1, down, nz - 1)):
            p = t - HOP * far

            @pl.when(jnp.logical_and(p >= 0, p < pieces))
            def _(way=way, far=far, step=step, p=p):
                k, i = p // ncol, p % ncol
                piece = gath.at[way, k, i]
                landed(piece, got.at[way, k, i])

                @pl.when(far < nz - 1)
                def _():
                    remote(piece, piece, fwd_sem.at[way], got.at[way, k, i], z_peer(step)).start()

                rows = rows_of(i * rb + way * half, half)
                fh[k, rows, :], fl[k, rows, :] = split(gath[way, k, i])

    m = rb * ncol // 4
    mine_rows = rb * ncol // 2

    def product(k, h):
        rows = rows_of(h * m, m)
        left_h, left_l = ih[rows, :], il[rows, :]
        right_h, right_l = fh[k], fl[k]
        total = jnp.dot(left_h, right_h, preferred_element_type=F32)
        total += jnp.dot(left_h, right_l, preferred_element_type=F32)
        total += jnp.dot(left_l, right_h, preferred_element_type=F32)
        part[k, rows, :] = total

    def rc_send(k):
        remote(part.at[k, rows_of((1 - core) * mine_rows, mine_rows)], rc.at[k], rc_s, rc_r.at[k], sibling).start()

    core_base = core * mine_rows
    x_rows = mine_rows // xln

    def rx_stage(k):
        landed(rc.at[k], rc_r.at[k])
        own = rows_of(core_base, mine_rows)
        part[k, own, :] += rc[k]
        if xln > 1:
            remote(part.at[k, rows_of(core_base + (1 - xl) * x_rows, x_rows)], rx.at[k], rx_s, rx_r.at[k], x_next).start()

    def ry_stage(k):
        base = core_base + xl * x_rows
        if xln > 1:
            landed(rx.at[k], rx_r.at[k])
            own = rows_of(base, x_rows)
            part[k, own, :] += rx[k]
        for j in range(1, ny):
            rows = rows_of(base + lax.rem(y + j, ny) * rb, rb)
            remote(part.at[k, rows], ry.at[k, j - 1], ry_s, ry_r.at[k], y_peer(j)).start()

    def dot_stage(k):
        landed(ry.at[k], ry_r.at[k])
        total = part[k, rows_of(core_base + xl * x_rows + y * rb, rb), :]
        for j in range(ny - 1):
            total += ry[k, j]
        panel_ref[k] = -total
        right_h, right_l = split(total)
        update = jnp.dot(fth[...], right_h, preferred_element_type=F32)
        update += jnp.dot(fth[...], right_l, preferred_element_type=F32)
        update += jnp.dot(ftl[...], right_h, preferred_element_type=F32)
        dpart[k] = update
        remote(dpart.at[k, rows_of((1 - core) * d_half, d_half)], dc.at[k], dc_s, dc_r.at[k], sibling).start()

    def dy_stage(k):
        landed(dc.at[k], dc_r.at[k])
        dpart[k, rows_of(core * d_half, d_half), :] += dc[k]
        for j in range(1, ny):
            rows = rows_of(core * d_half + lax.rem(y + j, ny) * d_y, d_y)
            remote(dpart.at[k, rows], dy.at[k, j - 1], dy_s, dy_r.at[k], y_peer(j)).start()

    def dx_stage(k):
        landed(dy.at[k], dy_r.at[k])
        own = rows_of(y_base, d_y)
        dpart[k, own, :] += functools.reduce(lambda a, b: a + b, [dy[k, j] for j in range(ny - 1)])
        for j in range(1, nx):
            rows = rows_of(y_base + lax.rem(x + j, nx) * d_x, d_x)
            remote(dpart.at[k, rows], dx.at[k, j - 1], dx_s, dx_r.at[k], x_peer(j)).start()

    def dz_stage(k):
        landed(dx.at[k], dx_r.at[k])
        own = rows_of(x_base, d_x)
        dpart[k, own, :] += functools.reduce(lambda a, b: a + b, [dx[k, j] for j in range(nx - 1)])
        for j in range(1, nz):
            rows, cols = z_place(lax.rem(z + j, nz))
            remote(dpart.at[k, rows, cols], dz.at[k, j - 1], dz_s, dz_r.at[k], z_peer(j)).start()

    def az_stage(k):
        landed(dz.at[k], dz_r.at[k])
        total = dpart[k, z_rows, z_lanes] + dinv[k]
        for j in range(nz - 1):
            total += dz[k, j]
        full[k, z_rows, z_lanes] = total
        place = full.at[k, z_rows, z_lanes]
        for j in range(1, nz):
            remote(place, place, az_s, az_r.at[k], z_peer(j)).start()

    def ax_stage(k):
        landed(dz.at[k], az_r.at[k])
        place = full.at[k, rows_of(x_base, d_x)]
        for j in range(1, nx):
            remote(place, place, ax_s, ax_r.at[k], x_peer(j)).start()

    def ay_stage(k):
        landed(dx.at[k], ax_r.at[k])
        place = full.at[k, rows_of(y_base, d_y)]
        for j in range(1, ny):
            remote(place, place, ay_s, ay_r.at[k], y_peer(j)).start()

    def ac_stage(k):
        landed(dy.at[k], ay_r.at[k])
        place = full.at[k, rows_of(core * d_half, d_half)]
        remote(place, place, ac_s, ac_r.at[k], sibling).start()

    def out_copy(k):
        cols = pl.ds(pl.multiple_of(k * ch, ch), ch)
        return pltpu.make_async_copy(full.at[k], diag_hbm.at[:, cols], out_sem.at[k])

    def out_stage(k):
        landed(dc.at[k], ac_r.at[k])
        out_copy(k).start()

    for k in range(chunks):
        dinv_copy(k).wait()

    stages = {
        "rx": rx_stage, "ry": ry_stage, "dot": dot_stage, "dy": dy_stage, "dx": dx_stage, "dz": dz_stage,
        "az": az_stage, "ax": ax_stage, "ay": ay_stage, "ac": ac_stage, "out": out_stage,
    }
    masks = rb * ncol // 32 // 4

    ready = (ncol - 1 + HOP * (nz - 1)) // per + 1

    @pl.loop(0, 4 * chunks + ready + 3 + STAGES["out"])
    def _(u):
        @pl.when(u < 4 * (chunks - 1) + ready)
        def _():
            pl.when(jnp.logical_and(u % 4 == 0, u // 4 + 2 < chunks))(lambda: send_source(u // 4 + 2))

            @pl.loop(0, per)
            def _(n):
                gather_step(u * per + n)

        @pl.when(u < 4)
        def _():
            @pl.loop(0, masks)
            def _(n):
                mask_rows(u * masks + n)

        since = u - ready

        @pl.when(jnp.logical_and(since >= 0, since < 4 * chunks))
        def _():
            product(since // 4, since % 4)
            pl.when(since % 4 == 3)(lambda: rc_send(since // 4))

        for name, after in sorted(STAGES.items(), key=lambda item: -item[1]):
            since = u - ready - 3 - after
            runs = jnp.logical_and(since % 4 == 0, jnp.logical_and(since >= 0, since < 4 * chunks))
            pl.when(runs)(lambda name=name, since=since: stages[name](since // 4))

    for k in range(chunks):
        out_copy(k).wait()
    sent(fac_ref, src_sem)
    pl.when(jnp.logical_not(on_diag))(lambda: sent(fac_ref, src_sem))
    pl.when(up < nz - 1)(lambda: sent(gath.at[0], fwd_sem.at[0]))
    pl.when(down < nz - 1)(lambda: sent(gath.at[1], fwd_sem.at[1]))
    sent(rc, rc_s)
    if xln > 1:
        sent(rx, rx_s)
    for ref, sem in ((ry, ry_s), (dc, dc_s), (dy, dy_s), (dx, dx_s), (dz, dz_s), (dz, az_s), (dx, ax_s), (dy, ay_s), (dc, ac_s)):
        sent(ref, sem)


def make(g):
    nz, xhn, xln, ny, w, ch, rb = (g[k] for k in ("NZ", "XH", "XL", "NY", "W", "CH", "RB"))
    nx, chunks, ncol = xhn * xln, w // ch, xln * ny * 2
    n = rb * ncol
    dma = pltpu.SemaphoreType.DMA
    d_half, d_y, d_x = w // 2, w // 2 // ny, w // 2 // ny // nx
    d_z = d_x * (ch // 128) // nz

    def body(inverse, pattern, factor, diag_inverse):
        panel, diag = pl.pallas_call(
            functools.partial(kernel, g),
            out_shape=(jax.ShapeDtypeStruct((chunks, rb, ch), F32), jax.ShapeDtypeStruct((w, w), F32)),
            in_specs=[
                pl.BlockSpec(memory_space=pl.ANY),
                pl.BlockSpec(memory_space=pltpu.SMEM),
                pl.BlockSpec(memory_space=pltpu.VMEM),
                pl.BlockSpec(memory_space=pl.ANY),
            ],
            out_specs=(pl.BlockSpec(memory_space=pltpu.VMEM), pl.BlockSpec(memory_space=pl.ANY)),
            scratch_shapes=[
                pltpu.VMEM((n, n), F32),
                pltpu.VMEM((n, n), BF16),
                pltpu.VMEM((n, n), BF16),
                pltpu.VMEM((2, chunks, ncol, rb // 2, ch), F32),
                pltpu.VMEM((chunks, n, ch), BF16),
                pltpu.VMEM((chunks, n, ch), BF16),
                pltpu.VMEM((chunks, n, ch), F32),
                pltpu.VMEM((chunks, n // 2, ch), F32),
                pltpu.VMEM((chunks, n // 2 // xln, ch), F32),
                pltpu.VMEM((chunks, ny - 1, rb, ch), F32),
                pltpu.VMEM((w, rb), BF16),
                pltpu.VMEM((w, rb), BF16),
                pltpu.VMEM((chunks, w, ch), F32),
                pltpu.VMEM((chunks, d_half, ch), F32),
                pltpu.VMEM((chunks, ny - 1, d_y, ch), F32),
                pltpu.VMEM((chunks, nx - 1, d_x, ch), F32),
                pltpu.VMEM((chunks, nz - 1, d_z, 128), F32),
                pltpu.VMEM((chunks, w, ch), F32),
                pltpu.VMEM((chunks, d_z, 128), F32),
                dma((1 + chunks,)),
                dma((2, chunks, ncol)),
                dma,
                dma((2,)),
            ]
            + [dma, dma((chunks,))] * 11
            + [dma((chunks,))],
            compiler_params=pltpu.CompilerParams(
                collective_id=0, has_side_effects=True, vmem_limit_bytes=63 * 2**20
            ),
        )(inverse, pattern, factor, diag_inverse)
        return panel.transpose(1, 0, 2).reshape(rb, w), diag

    return body


def solution(mesh):
    return jax.shard_map(
        make(FULL),
        mesh=mesh,
        in_specs=(P("row", "col"), P(), P(("row", "col"), None), P()),
        out_specs=(P(("row", "col"), None), P()),
        check_vma=False,
    )
```

```python
import functools

import jax
import jax.numpy as jnp
from jax import lax
from jax.experimental import pallas as pl
from jax.experimental.pallas import tpu as pltpu
from jax.sharding import PartitionSpec as P

MESH = pl.DeviceIdType.MESH
F32 = jnp.float32
BF16 = jnp.bfloat16

FULL = {"NZ": 8, "XH": 2, "XL": 2, "NY": 4, "W": 1024, "CH": 128, "RB": 96, "B": 512}
STAGES = {"ry": 1, "dot": 5, "dp": 7, "dz": 10, "ap": 12, "ac": 15, "out": 16}
HOP = 4
AHEAD = 1


def split(value):
    high = value.astype(BF16)
    return high, (value - high.astype(F32)).astype(BF16)


def kernel(
    g, inv_hbm, pat_ref, fac_ref, dinv_hbm, panel_ref, diag_hbm,
    stage, ih, il, gath, fh, fl, part, rc, ry, fth, ftl, dpart, dc, dp, dz, full, dinv,
    load_sem, got, src_sem, fwd_sem, rc_s, rc_r, ry_s, ry_r, dc_s, dc_r, dp_s, dp_r,
    dz_s, dz_r, ap_s, ap_r, ac_s, ac_r, out_sem,
):
    nz, xhn, xln, ny, w, ch, rb = (g[k] for k in ("NZ", "XH", "XL", "NY", "W", "CH", "RB"))
    nx, chunks, ncol = xhn * xln, w // ch, xln * ny * 2
    per_way = ncol // 2
    row, col = lax.axis_index("row"), lax.axis_index("col")
    z, xh = row // xhn, row % xhn
    core, y, xl = col % 2, (col // 2) % ny, col // (2 * ny)
    x = xh * xln + xl

    def at(z_, x_, y_, core_):
        return (z_ * xhn + x_ // xln, (x_ % xln) * (2 * ny) + y_ * 2 + core_)

    def z_peer(j):
        return at(lax.rem(z + j, nz), x, y, core)

    def plane_peer(j):
        return at(z, lax.rem(x + j // ny, nx), lax.rem(y + j % ny, ny), core)

    def row_peer(j):
        return at(z, xh * xln + lax.rem(xl + j // ny, xln), lax.rem(y + j % ny, ny), core)

    sibling = at(z, x, y, 1 - core)
    z_root = col // 2
    up = lax.rem(z - z_root + nz, nz)
    down = lax.rem(nz - up, nz)
    is_root = up == 0
    on_diag = row == col

    def remote(src, dst, send, recv, dev):
        return pltpu.make_async_remote_copy(
            src_ref=src, dst_ref=dst, send_sem=send, recv_sem=recv, device_id=dev, device_id_type=MESH
        )

    def landed(ref, recv):
        remote(ref, ref, recv, recv, sibling).wait_recv()

    def sent(ref, send):
        remote(ref, ref, send, send, sibling).wait_send()

    load = pltpu.make_async_copy(inv_hbm, stage, load_sem.at[0])
    load.start()
    d_half, d_rows = w // 2, w // 2 // (nx * ny)

    def rows_of(first, size):
        return pl.ds(pl.multiple_of(first, size), size)

    mine_d = rows_of(core * d_half + (x * ny + y) * d_rows, d_rows)

    def dinv_copy(k):
        cols = pl.ds(pl.multiple_of(k * ch, ch), ch)
        return pltpu.make_async_copy(dinv_hbm.at[mine_d, cols], dinv.at[k], load_sem.at[1 + k])

    for k in range(chunks):
        dinv_copy(k).start()

    barrier = pltpu.get_barrier_semaphore()

    def greet(dev):
        pl.semaphore_signal(barrier, inc=1, device_id=dev, device_id_type=MESH)

    greet(sibling)
    for j in range(1, nz):
        greet(z_peer(j))
    for j in range(1, nx * ny):
        greet(plane_peer(j))
    others = 1 + (nz - 1) + (nx * ny - 1)
    for a in range(xhn):
        pl.when(jnp.logical_not(jnp.logical_and(on_diag, xh == a)))(lambda a=a: greet((z * xhn + a, row)))

    @pl.when(is_root)
    def _():
        @pl.loop(0, ncol)
        def _(j):
            pl.when(jnp.logical_not(jnp.logical_and(on_diag, j == col)))(lambda: greet((z * xhn + core, j)))

    mine = jnp.where(on_diag, 1, 0)
    pl.semaphore_wait(barrier, others + xhn - mine + jnp.where(is_root, ncol - mine, 0))

    def send_source(k):
        src = fac_ref.at[:, pl.ds(pl.multiple_of(k * ch, ch), ch)]
        dst = gath.at[k, col]
        for a in range(xhn):
            here = jnp.logical_and(on_diag, xh == a)
            pl.when(jnp.logical_not(here))(
                lambda a=a: remote(src, dst, src_sem, got.at[k, col], (z * xhn + a, row)).start()
            )
            pl.when(here)(lambda: pltpu.make_async_copy(src, dst, got.at[k, col]).start())

    for k in range(min(AHEAD, chunks)):
        send_source(k)
    turned = fac_ref[...].T
    fth[...], ftl[...] = split(turned)
    load.wait()

    def mask_rows(i):
        block, part_of = i // (rb // 32), i % (rb // 32)
        dest = rows_of(((block % 2) * (ncol // 2) + block // 2) * rb + part_of * 32, 32)
        tiles = (rb * ncol) // g["B"]
        tile_row = (i * 32) // g["B"]
        for j in range(tiles):
            keep = pat_ref[row * tiles + tile_row, col * tiles + j].astype(F32)
            cols = pl.ds(j * g["B"], g["B"])
            ih[dest, cols], il[dest, cols] = split(stage[rows_of(i * 32, 32), cols] * keep)


    pieces = chunks * per_way

    def gather_step(t):
        for way, far, step in ((0, up, 1), (1, down, nz - 1)):
            p = t - HOP * far

            @pl.when(jnp.logical_and(p >= 0, p < pieces))
            def _(way=way, far=far, step=step, p=p):
                k, i = p // per_way, way * per_way + p % per_way
                piece = gath.at[k, i]
                landed(piece, got.at[k, i])

                @pl.when(far < nz - 1)
                def _():
                    remote(piece, piece, fwd_sem.at[way], got.at[k, i], z_peer(step)).start()

                rows = rows_of(i * rb, rb)
                fh[k, rows, :], fl[k, rows, :] = split(gath[k, i])

    m = rb * ncol // 4
    mine_rows = rb * ncol // 2

    def product(k, h):
        rows = rows_of(h * m, m)
        left_h, left_l = ih[rows, :], il[rows, :]
        right_h, right_l = fh[k], fl[k]
        total = jnp.dot(left_h, right_h, preferred_element_type=F32)
        total += jnp.dot(left_h, right_l, preferred_element_type=F32)
        total += jnp.dot(left_l, right_h, preferred_element_type=F32)
        part[k, rows, :] = total

    def rc_send(k):
        remote(part.at[k, rows_of((1 - core) * mine_rows, mine_rows)], rc.at[k], rc_s, rc_r.at[k], sibling).start()

    core_base = core * mine_rows
    def ry_stage(k):
        landed(rc.at[k], rc_r.at[k])
        part[k, rows_of(core_base, mine_rows), :] += rc[k]
        for j in range(1, xln * ny):
            place = lax.rem(xl + j // ny, xln) * ny + lax.rem(y + j % ny, ny)
            rows = rows_of(core_base + place * rb, rb)
            remote(part.at[k, rows], ry.at[k, j - 1], ry_s, ry_r.at[k], row_peer(j)).start()

    def dot_stage(k):
        landed(ry.at[k], ry_r.at[k])
        total = part[k, rows_of(core_base + (xl * ny + y) * rb, rb), :]
        for j in range(xln * ny - 1):
            total += ry[k, j]
        panel_ref[k] = -total
        right_h, right_l = split(total)
        update = jnp.dot(fth[...], right_h, preferred_element_type=F32)
        update += jnp.dot(fth[...], right_l, preferred_element_type=F32)
        update += jnp.dot(ftl[...], right_h, preferred_element_type=F32)
        dpart[k] = update
        remote(dpart.at[k, rows_of((1 - core) * d_half, d_half)], dc.at[k], dc_s, dc_r.at[k], sibling).start()

    def dp_stage(k):
        landed(dc.at[k], dc_r.at[k])
        dpart[k, rows_of(core * d_half, d_half), :] += dc[k]
        for j in range(1, nx * ny):
            place = lax.rem(x + j // ny, nx) * ny + lax.rem(y + j % ny, ny)
            rows = rows_of(core * d_half + place * d_rows, d_rows)
            remote(dpart.at[k, rows], dp.at[k, j - 1], dp_s, dp_r.at[k], plane_peer(j)).start()

    def dz_stage(k):
        landed(dp.at[k], dp_r.at[k])
        total = dpart[k, mine_d, :]
        for j in range(nx * ny - 1):
            total += dp[k, j]
        dz[k, z] = total
        for j in range(1, nz):
            remote(dz.at[k, z], dz.at[k, z], dz_s, dz_r.at[k], z_peer(j)).start()

    def ap_stage(k):
        landed(dz.at[k, pl.ds(0, nz - 1)], dz_r.at[k])
        total = dinv[k]
        for j in range(nz):
            total += dz[k, j]
        full[k, mine_d, :] = total
        place = full.at[k, mine_d]
        for j in range(1, nx * ny):
            remote(place, place, ap_s, ap_r.at[k], plane_peer(j)).start()

    def ac_stage(k):
        landed(dp.at[k], ap_r.at[k])
        place = full.at[k, rows_of(core * d_half, d_half)]
        remote(place, place, ac_s, ac_r.at[k], sibling).start()

    def out_copy(k):
        cols = pl.ds(pl.multiple_of(k * ch, ch), ch)
        return pltpu.make_async_copy(full.at[k], diag_hbm.at[:, cols], out_sem.at[k])

    def out_stage(k):
        landed(dc.at[k], ac_r.at[k])
        out_copy(k).start()

    for k in range(chunks):
        dinv_copy(k).wait()

    stages = {
        "ry": ry_stage, "dot": dot_stage, "dp": dp_stage, "dz": dz_stage, "ap": ap_stage, "ac": ac_stage, "out": out_stage,
    }
    masks = rb * ncol // 32 // 4

    per = max(1, per_way // 4)
    ready = (per_way - 1 + HOP * (nz - 1)) // per + 1

    @pl.loop(0, 4 * chunks + ready + 3 + STAGES["out"])
    def _(u):
        @pl.when(u < 4 * (chunks - 1) + ready)
        def _():
            pl.when(jnp.logical_and(u % 4 == 0, u // 4 + AHEAD < chunks))(lambda: send_source(u // 4 + AHEAD))

            @pl.loop(0, per)
            def _(n):
                gather_step(u * per + n)

        @pl.when(u < 4)
        def _():
            @pl.loop(0, masks)
            def _(n):
                mask_rows(u * masks + n)

        since = u - ready

        @pl.when(jnp.logical_and(since >= 0, since < 4 * chunks))
        def _():
            product(since // 4, since % 4)
            pl.when(since % 4 == 3)(lambda: rc_send(since // 4))

        for name, after in sorted(STAGES.items(), key=lambda item: -item[1]):
            since = u - ready - 3 - after
            runs = jnp.logical_and(since % 4 == 0, jnp.logical_and(since >= 0, since < 4 * chunks))
            pl.when(runs)(lambda name=name, since=since: stages[name](since // 4))

    for k in range(chunks):
        out_copy(k).wait()
    sent(fac_ref, src_sem)
    pl.when(jnp.logical_not(on_diag))(lambda: sent(fac_ref, src_sem))
    pl.when(up < nz - 1)(lambda: sent(gath.at[:, pl.ds(0, per_way)], fwd_sem.at[0]))
    pl.when(down < nz - 1)(lambda: sent(gath.at[:, pl.ds(per_way, per_way)], fwd_sem.at[1]))
    sent(rc, rc_s)
    for ref, sem in ((ry, ry_s), (dc, dc_s), (dp, dp_s), (dz.at[:, pl.ds(0, nz - 1)], dz_s), (dp, ap_s), (dc, ac_s)):
        sent(ref, sem)


def make(g):
    nz, xhn, xln, ny, w, ch, rb = (g[k] for k in ("NZ", "XH", "XL", "NY", "W", "CH", "RB"))
    nx, chunks, ncol = xhn * xln, w // ch, xln * ny * 2
    n = rb * ncol
    dma = pltpu.SemaphoreType.DMA
    d_half, d_rows = w // 2, w // 2 // (nx * ny)

    def body(inverse, pattern, factor, diag_inverse):
        panel, diag = pl.pallas_call(
            functools.partial(kernel, g),
            out_shape=(jax.ShapeDtypeStruct((chunks, rb, ch), F32), jax.ShapeDtypeStruct((w, w), F32)),
            in_specs=[
                pl.BlockSpec(memory_space=pl.ANY),
                pl.BlockSpec(memory_space=pltpu.SMEM),
                pl.BlockSpec(memory_space=pltpu.VMEM),
                pl.BlockSpec(memory_space=pl.ANY),
            ],
            out_specs=(pl.BlockSpec(memory_space=pltpu.VMEM), pl.BlockSpec(memory_space=pl.ANY)),
            scratch_shapes=[
                pltpu.VMEM((n, n), F32),
                pltpu.VMEM((n, n), BF16),
                pltpu.VMEM((n, n), BF16),
                pltpu.VMEM((chunks, ncol, rb, ch), F32),
                pltpu.VMEM((chunks, n, ch), BF16),
                pltpu.VMEM((chunks, n, ch), BF16),
                pltpu.VMEM((chunks, n, ch), F32),
                pltpu.VMEM((chunks, n // 2, ch), F32),
                pltpu.VMEM((chunks, xln * ny - 1, rb, ch), F32),
                pltpu.VMEM((w, rb), BF16),
                pltpu.VMEM((w, rb), BF16),
                pltpu.VMEM((chunks, w, ch), F32),
                pltpu.VMEM((chunks, d_half, ch), F32),
                pltpu.VMEM((chunks, nx * ny - 1, d_rows, ch), F32),
                pltpu.VMEM((chunks, nz, d_rows, ch), F32),
                pltpu.VMEM((chunks, w, ch), F32),
                pltpu.VMEM((chunks, d_rows, ch), F32),
                dma((1 + chunks,)),
                dma((chunks, ncol)),
                dma,
                dma((2,)),
            ]
            + [dma, dma((chunks,))] * 7
            + [dma((chunks,))],
            compiler_params=pltpu.CompilerParams(
                collective_id=0, has_side_effects=True, vmem_limit_bytes=63 * 2**20
            ),
        )(inverse, pattern, factor, diag_inverse)
        return panel.transpose(1, 0, 2).reshape(rb, w), diag

    return body


def solution(mesh):
    return jax.shard_map(
        make(FULL),
        mesh=mesh,
        in_specs=(P("row", "col"), P(), P(("row", "col"), None), P()),
        out_specs=(P(("row", "col"), None), P()),
        check_vma=False,
    )
```

```python
import functools

import jax
import jax.numpy as jnp
from jax import lax
from jax.experimental import pallas as pl
from jax.experimental.pallas import tpu as pltpu
from jax.sharding import PartitionSpec as P

MESH = pl.DeviceIdType.MESH
F32 = jnp.float32
BF16 = jnp.bfloat16

FULL = {"NZ": 8, "XH": 2, "XL": 2, "NY": 4, "W": 1024, "CH": 128, "RB": 96, "B": 512}
STAGES = {"ry": 3, "dot": 9, "da": 12, "db": 17, "dz": 21, "ab": 25, "aa": 29, "ac": 34, "out": 37}
HOP = 4
AHEAD = 2
LAG = 2


def split(value):
    high = value.astype(BF16)
    return high, (value - high.astype(F32)).astype(BF16)


def kernel(
    g, inv_hbm, pat_ref, fac_ref, dinv_hbm, panel_ref, diag_hbm,
    stage, ih, il, relayed, gath, fh, fl, part, rc, ry, fth, ftl, dpart, dc, da, db, dz, full, dinv,
    load_sem, got, relay_got, src_sem, relay_sem, fwd_sem, rc_s, rc_r, ry_s, ry_r, dc_s, dc_r, da_s, da_r, db_s, db_r,
    dz_s, dz_r, ab_s, ab_r, aa_s, aa_r, ac_s, ac_r, out_sem,
):
    nz, xhn, xln, ny, w, ch, rb = (g[k] for k in ("NZ", "XH", "XL", "NY", "W", "CH", "RB"))
    nx, chunks, ncol = xhn * xln, w // ch, xln * ny * 2
    per_way = ncol // 2
    row, col = lax.axis_index("row"), lax.axis_index("col")
    z, xh = row // xhn, row % xhn
    core, y, xl = col % 2, (col // 2) % ny, col // (2 * ny)
    x = xh * xln + xl

    def at(z_, x_, y_, core_):
        return (z_ * xhn + x_ // xln, (x_ % xln) * (2 * ny) + y_ * 2 + core_)

    def z_peer(j):
        return at(lax.rem(z + j, nz), x, y, core)

    def plane_peer(j):
        return at(z, lax.rem(x + j // ny, nx), lax.rem(y + j % ny, ny), core)

    def x_peer(j):
        return at(z, lax.rem(x + j, nx), y, core)

    def y_peer(j):
        return at(z, x, lax.rem(y + j, ny), core)

    def row_peer(j):
        return at(z, xh * xln + lax.rem(xl + j // ny, xln), lax.rem(y + j % ny, ny), core)

    sibling = at(z, x, y, 1 - core)
    z_root = col // 2
    up = lax.rem(z - z_root + nz, nz)
    down = lax.rem(nz - up, nz)
    is_root = up == 0
    on_diag = row == col
    is_relay = jnp.logical_and(y == lax.rem(z, ny), core == xh)
    own_relay = (row, xl * (2 * ny) + lax.rem(z, ny) * 2 + xh)

    def remote(src, dst, send, recv, dev):
        return pltpu.make_async_remote_copy(
            src_ref=src, dst_ref=dst, send_sem=send, recv_sem=recv, device_id=dev, device_id_type=MESH
        )

    def landed(ref, recv):
        remote(ref, ref, recv, recv, sibling).wait_recv()

    def sent(ref, send):
        remote(ref, ref, send, send, sibling).wait_send()

    load = pltpu.make_async_copy(inv_hbm, stage, load_sem.at[0])
    load.start()
    d_half, d_a, d_rows = w // 2, w // 2 // ny, w // 2 // (nx * ny)

    def rows_of(first, size):
        return pl.ds(pl.multiple_of(first, size), size)

    y_base = core * d_half + y * d_a
    mine_d = rows_of(y_base + x * d_rows, d_rows)

    def dinv_copy(k):
        cols = pl.ds(pl.multiple_of(k * ch, ch), ch)
        return pltpu.make_async_copy(dinv_hbm.at[mine_d, cols], dinv.at[k], load_sem.at[1 + k])

    for k in range(chunks):
        dinv_copy(k).start()

    barrier = pltpu.get_barrier_semaphore()

    def greet(dev):
        pl.semaphore_signal(barrier, inc=1, device_id=dev, device_id_type=MESH)

    greet(sibling)
    for j in range(1, nz):
        greet(z_peer(j))
    for j in range(1, nx * ny):
        greet(plane_peer(j))
    others = 1 + (nz - 1) + (nx * ny - 1)
    pl.when(jnp.logical_not(is_relay))(lambda: greet(own_relay))

    @pl.when(is_relay)
    def _():
        for j in range(2 * ny):
            other = xl * (2 * ny) + j
            pl.when(other != col)(lambda other=other: greet((row, other)))
        for a in range(xhn):
            pl.when(jnp.logical_not(jnp.logical_and(on_diag, xh == a)))(lambda a=a: greet((z * xhn + a, row)))

    @pl.when(is_root)
    def _():
        for j in range(xln):
            other = j * (2 * ny) + y * 2 + core
            pl.when(jnp.logical_not(jnp.logical_and(on_diag, other == col)))(
                lambda other=other: greet((z * xhn + core, other))
            )

    mine = jnp.where(on_diag, 1, 0)
    feed = jnp.where(is_relay, 2 * ny - 1 + xhn - mine, 1) + jnp.where(is_root, xln - mine, 0)
    pl.semaphore_wait(barrier, others + feed)

    def send_source(k):
        src = fac_ref.at[:, pl.ds(pl.multiple_of(k * ch, ch), ch)]
        dst, arrives = relayed.at[k, y * 2 + core], relay_got.at[k, y * 2 + core]
        pl.when(jnp.logical_not(is_relay))(lambda: remote(src, dst, src_sem, arrives, own_relay).start())
        pl.when(is_relay)(lambda: pltpu.make_async_copy(src, dst, arrives).start())

    def relay_step(t):
        k, i = t // per_way, t % per_way
        piece, place = relayed.at[k, i], xl * (2 * ny) + i

        @pl.when(is_relay)
        def _():
            landed(piece, relay_got.at[k, i])
            for a in range(xhn):
                here = jnp.logical_and(on_diag, xh == a)
                pl.when(jnp.logical_not(here))(
                    lambda a=a: remote(
                        piece, gath.at[k, place], relay_sem, got.at[k, place], (z * xhn + a, row)
                    ).start()
                )
                pl.when(here)(lambda: pltpu.make_async_copy(piece, gath.at[k, place], got.at[k, place]).start())

    for k in range(min(AHEAD, chunks)):
        send_source(k)
    turned = fac_ref[...].T
    fth[...], ftl[...] = split(turned)
    load.wait()

    def mask_rows(i):
        block, part_of = i // (rb // 32), i % (rb // 32)
        dest = rows_of(((block % 2) * (ncol // 2) + block // 2) * rb + part_of * 32, 32)
        tiles = (rb * ncol) // g["B"]
        tile_row = (i * 32) // g["B"]
        for j in range(tiles):
            keep = pat_ref[row * tiles + tile_row, col * tiles + j].astype(F32)
            cols = pl.ds(j * g["B"], g["B"])
            ih[dest, cols], il[dest, cols] = split(stage[rows_of(i * 32, 32), cols] * keep)


    pieces = chunks * per_way

    def gather_step(t):
        for way, far, step in ((0, up, 1), (1, down, nz - 1)):
            p = t - HOP * far - LAG

            @pl.when(jnp.logical_and(p >= 0, p < pieces))
            def _(way=way, far=far, step=step, p=p):
                k, i = p // per_way, way * per_way + p % per_way
                piece = gath.at[k, i]
                landed(piece, got.at[k, i])

                @pl.when(far < nz - 1)
                def _():
                    remote(piece, piece, fwd_sem.at[way], got.at[k, i], z_peer(step)).start()

                rows = rows_of(i * rb, rb)
                fh[k, rows, :], fl[k, rows, :] = split(gath[k, i])

    m = rb * ncol // 4
    mine_rows = rb * ncol // 2

    def product(k, h):
        rows = rows_of(h * m, m)
        left_h, left_l = ih[rows, :], il[rows, :]
        right_h, right_l = fh[k], fl[k]
        total = jnp.dot(left_h, right_h, preferred_element_type=F32)
        total += jnp.dot(left_h, right_l, preferred_element_type=F32)
        total += jnp.dot(left_l, right_h, preferred_element_type=F32)
        part[k, rows, :] = total

    def rc_send(k):
        remote(part.at[k, rows_of((1 - core) * mine_rows, mine_rows)], rc.at[k], rc_s, rc_r.at[k], sibling).start()

    core_base = core * mine_rows
    def ry_stage(k):
        landed(rc.at[k], rc_r.at[k])
        part[k, rows_of(core_base, mine_rows), :] += rc[k]
        for j in range(1, xln * ny):
            place = lax.rem(xl + j // ny, xln) * ny + lax.rem(y + j % ny, ny)
            rows = rows_of(core_base + place * rb, rb)
            remote(part.at[k, rows], ry.at[k, j - 1], ry_s, ry_r.at[k], row_peer(j)).start()

    def dot_stage(k):
        landed(ry.at[k], ry_r.at[k])
        total = part[k, rows_of(core_base + (xl * ny + y) * rb, rb), :]
        for j in range(xln * ny - 1):
            total += ry[k, j]
        panel_ref[k] = -total
        right_h, right_l = split(total)
        update = jnp.dot(fth[...], right_h, preferred_element_type=F32)
        update += jnp.dot(fth[...], right_l, preferred_element_type=F32)
        update += jnp.dot(ftl[...], right_h, preferred_element_type=F32)
        dpart[k] = update
        remote(dpart.at[k, rows_of((1 - core) * d_half, d_half)], dc.at[k], dc_s, dc_r.at[k], sibling).start()

    def da_stage(k):
        landed(dc.at[k], dc_r.at[k])
        dpart[k, rows_of(core * d_half, d_half), :] += dc[k]
        for j in range(1, ny):
            rows = rows_of(core * d_half + lax.rem(y + j, ny) * d_a, d_a)
            remote(dpart.at[k, rows], da.at[k, j - 1], da_s, da_r.at[k], y_peer(j)).start()

    def db_stage(k):
        landed(da.at[k], da_r.at[k])
        total = dpart[k, rows_of(y_base, d_a), :]
        for j in range(ny - 1):
            total += da[k, j]
        dpart[k, rows_of(y_base, d_a), :] = total
        for j in range(1, nx):
            rows = rows_of(y_base + lax.rem(x + j, nx) * d_rows, d_rows)
            remote(dpart.at[k, rows], db.at[k, j - 1], db_s, db_r.at[k], x_peer(j)).start()

    def dz_stage(k):
        landed(db.at[k], db_r.at[k])
        total = dpart[k, mine_d, :]
        for j in range(nx - 1):
            total += db[k, j]
        dz[k, z] = total
        for j in range(1, nz):
            remote(dz.at[k, z], dz.at[k, z], dz_s, dz_r.at[k], z_peer(j)).start()

    def ab_stage(k):
        landed(dz.at[k, pl.ds(0, nz - 1)], dz_r.at[k])
        total = dinv[k]
        for j in range(nz):
            total += dz[k, j]
        full[k, mine_d, :] = total
        place = full.at[k, mine_d]
        for j in range(1, nx):
            remote(place, place, ab_s, ab_r.at[k], x_peer(j)).start()

    def aa_stage(k):
        landed(db.at[k], ab_r.at[k])
        place = full.at[k, rows_of(y_base, d_a)]
        for j in range(1, ny):
            remote(place, place, aa_s, aa_r.at[k], y_peer(j)).start()

    def ac_stage(k):
        landed(da.at[k], aa_r.at[k])
        place = full.at[k, rows_of(core * d_half, d_half)]
        remote(place, place, ac_s, ac_r.at[k], sibling).start()

    def out_copy(k):
        cols = pl.ds(pl.multiple_of(k * ch, ch), ch)
        return pltpu.make_async_copy(full.at[k], diag_hbm.at[:, cols], out_sem.at[k])

    def out_stage(k):
        landed(dc.at[k], ac_r.at[k])
        out_copy(k).start()

    for k in range(chunks):
        dinv_copy(k).wait()

    stages = {
        "ry": ry_stage, "dot": dot_stage, "da": da_stage, "db": db_stage, "dz": dz_stage,
        "ab": ab_stage, "aa": aa_stage, "ac": ac_stage, "out": out_stage,
    }
    masks = rb * ncol // 32 // 4

    per = max(1, per_way // 4)
    ready = (per_way - 1 + HOP * (nz - 1) + LAG) // per + 1

    @pl.loop(0, 4 * chunks + ready + 3 + STAGES["out"])
    def _(u):
        @pl.when(u < 4 * (chunks - 1) + ready)
        def _():
            pl.when(jnp.logical_and(u % 4 == 0, u // 4 + AHEAD < chunks))(lambda: send_source(u // 4 + AHEAD))

            @pl.loop(0, per)
            def _(n):
                pl.when(u * per + n < pieces)(lambda: relay_step(u * per + n))
                gather_step(u * per + n)

        @pl.when(u < 4)
        def _():
            @pl.loop(0, masks)
            def _(n):
                mask_rows(u * masks + n)

        since = u - ready

        @pl.when(jnp.logical_and(since >= 0, since < 4 * chunks))
        def _():
            product(since // 4, since % 4)
            pl.when(since % 4 == 3)(lambda: rc_send(since // 4))

        for name, after in sorted(STAGES.items(), key=lambda item: -item[1]):
            since = u - ready - 3 - after
            runs = jnp.logical_and(since % 4 == 0, jnp.logical_and(since >= 0, since < 4 * chunks))
            pl.when(runs)(lambda name=name, since=since: stages[name](since // 4))

    for k in range(chunks):
        out_copy(k).wait()
    pl.when(jnp.logical_not(is_relay))(lambda: sent(fac_ref, src_sem))
    pl.when(is_relay)(lambda: sent(relayed, relay_sem))
    pl.when(jnp.logical_and(is_relay, jnp.logical_not(on_diag)))(lambda: sent(relayed, relay_sem))
    pl.when(up < nz - 1)(lambda: sent(gath.at[:, pl.ds(0, per_way)], fwd_sem.at[0]))
    pl.when(down < nz - 1)(lambda: sent(gath.at[:, pl.ds(per_way, per_way)], fwd_sem.at[1]))
    sent(rc, rc_s)
    for ref, sem in ((ry, ry_s), (dc, dc_s), (da, da_s), (db, db_s), (db, ab_s), (da, aa_s), (dc, ac_s)):
        sent(ref, sem)
    sent(dz.at[:, pl.ds(0, nz - 1)], dz_s)


def make(g):
    nz, xhn, xln, ny, w, ch, rb = (g[k] for k in ("NZ", "XH", "XL", "NY", "W", "CH", "RB"))
    nx, chunks, ncol = xhn * xln, w // ch, xln * ny * 2
    n = rb * ncol
    dma = pltpu.SemaphoreType.DMA
    d_half, d_a, d_rows = w // 2, w // 2 // ny, w // 2 // (nx * ny)

    def body(inverse, pattern, factor, diag_inverse):
        panel, diag = pl.pallas_call(
            functools.partial(kernel, g),
            out_shape=(jax.ShapeDtypeStruct((chunks, rb, ch), F32), jax.ShapeDtypeStruct((w, w), F32)),
            in_specs=[
                pl.BlockSpec(memory_space=pl.ANY),
                pl.BlockSpec(memory_space=pltpu.SMEM),
                pl.BlockSpec(memory_space=pltpu.VMEM),
                pl.BlockSpec(memory_space=pl.ANY),
            ],
            out_specs=(pl.BlockSpec(memory_space=pltpu.VMEM), pl.BlockSpec(memory_space=pl.ANY)),
            scratch_shapes=[
                pltpu.VMEM((n, n), F32),
                pltpu.VMEM((n, n), BF16),
                pltpu.VMEM((n, n), BF16),
                pltpu.VMEM((chunks, 2 * ny, rb, ch), F32),
                pltpu.VMEM((chunks, ncol, rb, ch), F32),
                pltpu.VMEM((chunks, n, ch), BF16),
                pltpu.VMEM((chunks, n, ch), BF16),
                pltpu.VMEM((chunks, n, ch), F32),
                pltpu.VMEM((chunks, n // 2, ch), F32),
                pltpu.VMEM((chunks, xln * ny - 1, rb, ch), F32),
                pltpu.VMEM((w, rb), BF16),
                pltpu.VMEM((w, rb), BF16),
                pltpu.VMEM((chunks, w, ch), F32),
                pltpu.VMEM((chunks, d_half, ch), F32),
                pltpu.VMEM((chunks, ny - 1, d_a, ch), F32),
                pltpu.VMEM((chunks, nx - 1, d_rows, ch), F32),
                pltpu.VMEM((chunks, nz, d_rows, ch), F32),
                pltpu.VMEM((chunks, w, ch), F32),
                pltpu.VMEM((chunks, d_rows, ch), F32),
                dma((1 + chunks,)),
                dma((chunks, ncol)),
                dma((chunks, 2 * ny)),
                dma,
                dma,
                dma((2,)),
            ]
            + [dma, dma((chunks,))] * 9
            + [dma((chunks,))],
            compiler_params=pltpu.CompilerParams(
                collective_id=0, has_side_effects=True, vmem_limit_bytes=63 * 2**20
            ),
        )(inverse, pattern, factor, diag_inverse)
        return panel.transpose(1, 0, 2).reshape(rb, w), diag

    return body


def solution(mesh):
    return jax.shard_map(
        make(FULL),
        mesh=mesh,
        in_specs=(P("row", "col"), P(), P(("row", "col"), None), P()),
        out_specs=(P(("row", "col"), None), P()),
        check_vma=False,
    )
```

```python
import functools

import jax
import jax.numpy as jnp
from jax import lax
from jax.experimental import pallas as pl
from jax.experimental.pallas import tpu as pltpu
from jax.sharding import PartitionSpec as P

MESH = pl.DeviceIdType.MESH
F32 = jnp.float32
BF16 = jnp.bfloat16

FULL = {"NZ": 8, "XH": 2, "XL": 2, "NY": 4, "W": 1024, "CH": 128, "RB": 96, "B": 512}
STAGES = {"ry": 3, "dot": 9, "da": 12, "db": 17, "dz": 21, "ab": 25, "aa": 29, "ac": 34, "out": 37}
HOP = 4
AHEAD = 1
LAG = 2


def split(value):
    high = value.astype(BF16)
    return high, (value - high.astype(F32)).astype(BF16)


def kernel(
    g, inv_hbm, pat_ref, fac_ref, dinv_hbm, panel_ref, diag_hbm,
    stage, ih, il, relayed, gath, fh, fl, part, rc, ry, fth, ftl, dpart, dc, da, db, dz, full, dinv,
    load_sem, got, relay_got, src_sem, relay_sem, fwd_sem, rc_s, rc_r, ry_s, ry_r, dc_s, dc_r, da_s, da_r, db_s, db_r,
    dz_s, dz_r, ab_s, ab_r, aa_s, aa_r, ac_s, ac_r, out_sem,
):
    nz, xhn, xln, ny, w, ch, rb = (g[k] for k in ("NZ", "XH", "XL", "NY", "W", "CH", "RB"))
    nx, chunks, ncol = xhn * xln, w // ch, xln * ny * 2
    per_way = ncol // 2
    row, col = lax.axis_index("row"), lax.axis_index("col")
    z, xh = row // xhn, row % xhn
    core, y, xl = col % 2, (col // 2) % ny, col // (2 * ny)
    x = xh * xln + xl

    def at(z_, x_, y_, core_):
        return (z_ * xhn + x_ // xln, (x_ % xln) * (2 * ny) + y_ * 2 + core_)

    def z_peer(j):
        return at(lax.rem(z + j, nz), x, y, core)

    def plane_peer(j):
        return at(z, lax.rem(x + j // ny, nx), lax.rem(y + j % ny, ny), core)

    def x_peer(j):
        return at(z, lax.rem(x + j, nx), y, core)

    def y_peer(j):
        return at(z, x, lax.rem(y + j, ny), core)

    def row_peer(j):
        return at(z, xh * xln + lax.rem(xl + j // ny, xln), lax.rem(y + j % ny, ny), core)

    sibling = at(z, x, y, 1 - core)
    z_root = col // 2
    up = lax.rem(z - z_root + nz, nz)
    down = lax.rem(nz - up, nz)
    is_root = up == 0
    on_diag = row == col
    is_relay = jnp.logical_and(y == lax.rem(z, ny), core == xh)
    own_relay = (row, xl * (2 * ny) + lax.rem(z, ny) * 2 + xh)

    def remote(src, dst, send, recv, dev):
        return pltpu.make_async_remote_copy(
            src_ref=src, dst_ref=dst, send_sem=send, recv_sem=recv, device_id=dev, device_id_type=MESH
        )

    def landed(ref, recv):
        remote(ref, ref, recv, recv, sibling).wait_recv()

    def sent(ref, send):
        remote(ref, ref, send, send, sibling).wait_send()

    load = pltpu.make_async_copy(inv_hbm, stage, load_sem.at[0])
    load.start()
    d_half, d_a, d_rows = w // 2, w // 2 // ny, w // 2 // (nx * ny)

    def rows_of(first, size):
        return pl.ds(pl.multiple_of(first, size), size)

    y_base = core * d_half + y * d_a
    mine_d = rows_of(y_base + x * d_rows, d_rows)

    def dinv_copy(k):
        cols = pl.ds(pl.multiple_of(k * ch, ch), ch)
        return pltpu.make_async_copy(dinv_hbm.at[mine_d, cols], dinv.at[k], load_sem.at[1 + k])

    for k in range(chunks):
        dinv_copy(k).start()

    barrier = pltpu.get_barrier_semaphore()

    def greet(dev):
        pl.semaphore_signal(barrier, inc=1, device_id=dev, device_id_type=MESH)

    greet(sibling)
    for j in range(1, nz):
        greet(z_peer(j))
    for j in range(1, nx * ny):
        greet(plane_peer(j))
    others = 1 + (nz - 1) + (nx * ny - 1)
    pl.when(jnp.logical_not(is_relay))(lambda: greet(own_relay))

    @pl.when(is_relay)
    def _():
        for j in range(2 * ny):
            other = xl * (2 * ny) + j
            pl.when(other != col)(lambda other=other: greet((row, other)))
        for a in range(xhn):
            pl.when(jnp.logical_not(jnp.logical_and(on_diag, xh == a)))(lambda a=a: greet((z * xhn + a, row)))

    @pl.when(is_root)
    def _():
        for j in range(xln):
            other = j * (2 * ny) + y * 2 + core
            pl.when(jnp.logical_not(jnp.logical_and(on_diag, other == col)))(
                lambda other=other: greet((z * xhn + core, other))
            )

    mine = jnp.where(on_diag, 1, 0)
    feed = jnp.where(is_relay, 2 * ny - 1 + xhn - mine, 1) + jnp.where(is_root, xln - mine, 0)
    pl.semaphore_wait(barrier, others + feed)

    def send_source(k):
        src = fac_ref.at[:, pl.ds(pl.multiple_of(k * ch, ch), ch)]
        dst, arrives = relayed.at[k, y * 2 + core], relay_got.at[k, y * 2 + core]
        pl.when(jnp.logical_not(is_relay))(lambda: remote(src, dst, src_sem, arrives, own_relay).start())
        pl.when(is_relay)(lambda: pltpu.make_async_copy(src, dst, arrives).start())

    def relay_step(t):
        k, i = t // per_way, t % per_way
        piece, place = relayed.at[k, i], xl * (2 * ny) + i

        @pl.when(is_relay)
        def _():
            landed(piece, relay_got.at[k, i])
            for a in range(xhn):
                here = jnp.logical_and(on_diag, xh == a)
                pl.when(jnp.logical_not(here))(
                    lambda a=a: remote(
                        piece, gath.at[k, place], relay_sem, got.at[k, place], (z * xhn + a, row)
                    ).start()
                )
                pl.when(here)(lambda: pltpu.make_async_copy(piece, gath.at[k, place], got.at[k, place]).start())

    for k in range(min(AHEAD, chunks)):
        send_source(k)
    turned = fac_ref[...].T
    fth[...], ftl[...] = split(turned)
    load.wait()

    def mask_rows(i):
        block, part_of = i // (rb // 32), i % (rb // 32)
        dest = rows_of(((block % 2) * (ncol // 2) + block // 2) * rb + part_of * 32, 32)
        tiles = (rb * ncol) // g["B"]
        tile_row = (i * 32) // g["B"]
        for j in range(tiles):
            keep = pat_ref[row * tiles + tile_row, col * tiles + j].astype(F32)
            cols = pl.ds(j * g["B"], g["B"])
            ih[dest, cols], il[dest, cols] = split(stage[rows_of(i * 32, 32), cols] * keep)


    pieces = chunks * per_way

    def gather_step(t):
        for way, far, step in ((0, up, 1), (1, down, nz - 1)):
            p = t - HOP * far - LAG

            @pl.when(jnp.logical_and(p >= 0, p < pieces))
            def _(way=way, far=far, step=step, p=p):
                k, i = p // per_way, way * per_way + p % per_way
                piece = gath.at[k, i]
                landed(piece, got.at[k, i])

                @pl.when(far < nz - 1)
                def _():
                    remote(piece, piece, fwd_sem.at[way], got.at[k, i], z_peer(step)).start()

                rows = rows_of(i * rb, rb)
                fh[k, rows, :], fl[k, rows, :] = split(gath[k, i])

    m = rb * ncol // 4
    mine_rows = rb * ncol // 2

    def product(k, h):
        rows = rows_of(h * m, m)
        left_h, left_l = ih[rows, :], il[rows, :]
        right_h, right_l = fh[k], fl[k]
        total = jnp.dot(left_h, right_h, preferred_element_type=F32)
        total += jnp.dot(left_h, right_l, preferred_element_type=F32)
        total += jnp.dot(left_l, right_h, preferred_element_type=F32)
        part[k, rows, :] = total

    def rc_send(k):
        remote(part.at[k, rows_of((1 - core) * mine_rows, mine_rows)], rc.at[k], rc_s, rc_r.at[k], sibling).start()

    core_base = core * mine_rows
    def ry_stage(k):
        landed(rc.at[k], rc_r.at[k])
        part[k, rows_of(core_base, mine_rows), :] += rc[k]
        for j in range(1, xln * ny):
            place = lax.rem(xl + j // ny, xln) * ny + lax.rem(y + j % ny, ny)
            rows = rows_of(core_base + place * rb, rb)
            remote(part.at[k, rows], ry.at[k, j - 1], ry_s, ry_r.at[k], row_peer(j)).start()

    def dot_stage(k):
        landed(ry.at[k], ry_r.at[k])
        total = part[k, rows_of(core_base + (xl * ny + y) * rb, rb), :]
        for j in range(xln * ny - 1):
            total += ry[k, j]
        panel_ref[k] = -total
        right_h, right_l = split(total)
        update = jnp.dot(fth[...], right_h, preferred_element_type=F32)
        update += jnp.dot(fth[...], right_l, preferred_element_type=F32)
        update += jnp.dot(ftl[...], right_h, preferred_element_type=F32)
        dpart[k] = update
        remote(dpart.at[k, rows_of((1 - core) * d_half, d_half)], dc.at[k], dc_s, dc_r.at[k], sibling).start()

    def da_stage(k):
        landed(dc.at[k], dc_r.at[k])
        dpart[k, rows_of(core * d_half, d_half), :] += dc[k]
        for j in range(1, ny):
            rows = rows_of(core * d_half + lax.rem(y + j, ny) * d_a, d_a)
            remote(dpart.at[k, rows], da.at[k, j - 1], da_s, da_r.at[k], y_peer(j)).start()

    def db_stage(k):
        landed(da.at[k], da_r.at[k])
        total = dpart[k, rows_of(y_base, d_a), :]
        for j in range(ny - 1):
            total += da[k, j]
        dpart[k, rows_of(y_base, d_a), :] = total
        for j in range(1, nx):
            rows = rows_of(y_base + lax.rem(x + j, nx) * d_rows, d_rows)
            remote(dpart.at[k, rows], db.at[k, j - 1], db_s, db_r.at[k], x_peer(j)).start()

    def dz_stage(k):
        landed(db.at[k], db_r.at[k])
        total = dpart[k, mine_d, :]
        for j in range(nx - 1):
            total += db[k, j]
        dz[k, z] = total
        for j in range(1, nz):
            remote(dz.at[k, z], dz.at[k, z], dz_s, dz_r.at[k], z_peer(j)).start()

    def ab_stage(k):
        landed(dz.at[k, pl.ds(0, nz - 1)], dz_r.at[k])
        total = dinv[k]
        for j in range(nz):
            total += dz[k, j]
        full[k, mine_d, :] = total
        place = full.at[k, mine_d]
        for j in range(1, nx):
            remote(place, place, ab_s, ab_r.at[k], x_peer(j)).start()

    def aa_stage(k):
        landed(db.at[k], ab_r.at[k])
        place = full.at[k, rows_of(y_base, d_a)]
        for j in range(1, ny):
            remote(place, place, aa_s, aa_r.at[k], y_peer(j)).start()

    def ac_stage(k):
        landed(da.at[k], aa_r.at[k])
        place = full.at[k, rows_of(core * d_half, d_half)]
        remote(place, place, ac_s, ac_r.at[k], sibling).start()

    def out_copy(k):
        cols = pl.ds(pl.multiple_of(k * ch, ch), ch)
        return pltpu.make_async_copy(full.at[k], diag_hbm.at[:, cols], out_sem.at[k])

    def out_stage(k):
        landed(dc.at[k], ac_r.at[k])
        out_copy(k).start()

    for k in range(chunks):
        dinv_copy(k).wait()

    stages = {
        "ry": ry_stage, "dot": dot_stage, "da": da_stage, "db": db_stage, "dz": dz_stage,
        "ab": ab_stage, "aa": aa_stage, "ac": ac_stage, "out": out_stage,
    }
    masks = rb * ncol // 32 // 4

    per = max(1, per_way // 4)
    ready = (per_way - 1 + HOP * (nz - 1) + LAG) // per + 1

    @pl.loop(0, 4 * chunks + ready + 3 + STAGES["out"])
    def _(u):
        @pl.when(u < 4 * (chunks - 1) + ready)
        def _():
            pl.when(jnp.logical_and(u % 4 == 0, u // 4 + AHEAD < chunks))(lambda: send_source(u // 4 + AHEAD))

            @pl.loop(0, per)
            def _(n):
                pl.when(u * per + n < pieces)(lambda: relay_step(u * per + n))
                gather_step(u * per + n)

        @pl.when(u < 4)
        def _():
            @pl.loop(0, masks)
            def _(n):
                mask_rows(u * masks + n)

        since = u - ready

        @pl.when(jnp.logical_and(since >= 0, since < 4 * chunks))
        def _():
            product(since // 4, since % 4)
            pl.when(since % 4 == 3)(lambda: rc_send(since // 4))

        for name, after in sorted(STAGES.items(), key=lambda item: -item[1]):
            since = u - ready - 3 - after
            runs = jnp.logical_and(since % 4 == 0, jnp.logical_and(since >= 0, since < 4 * chunks))
            pl.when(runs)(lambda name=name, since=since: stages[name](since // 4))

    for k in range(chunks):
        out_copy(k).wait()
    pl.when(jnp.logical_not(is_relay))(lambda: sent(fac_ref, src_sem))
    pl.when(is_relay)(lambda: sent(relayed, relay_sem))
    pl.when(jnp.logical_and(is_relay, jnp.logical_not(on_diag)))(lambda: sent(relayed, relay_sem))
    pl.when(up < nz - 1)(lambda: sent(gath.at[:, pl.ds(0, per_way)], fwd_sem.at[0]))
    pl.when(down < nz - 1)(lambda: sent(gath.at[:, pl.ds(per_way, per_way)], fwd_sem.at[1]))
    sent(rc, rc_s)
    for ref, sem in ((ry, ry_s), (dc, dc_s), (da, da_s), (db, db_s), (db, ab_s), (da, aa_s), (dc, ac_s)):
        sent(ref, sem)
    sent(dz.at[:, pl.ds(0, nz - 1)], dz_s)


def make(g):
    nz, xhn, xln, ny, w, ch, rb = (g[k] for k in ("NZ", "XH", "XL", "NY", "W", "CH", "RB"))
    nx, chunks, ncol = xhn * xln, w // ch, xln * ny * 2
    n = rb * ncol
    dma = pltpu.SemaphoreType.DMA
    d_half, d_a, d_rows = w // 2, w // 2 // ny, w // 2 // (nx * ny)

    def body(inverse, pattern, factor, diag_inverse):
        panel, diag = pl.pallas_call(
            functools.partial(kernel, g),
            out_shape=(jax.ShapeDtypeStruct((chunks, rb, ch), F32), jax.ShapeDtypeStruct((w, w), F32)),
            in_specs=[
                pl.BlockSpec(memory_space=pl.ANY),
                pl.BlockSpec(memory_space=pltpu.SMEM),
                pl.BlockSpec(memory_space=pltpu.VMEM),
                pl.BlockSpec(memory_space=pl.ANY),
            ],
            out_specs=(pl.BlockSpec(memory_space=pltpu.VMEM), pl.BlockSpec(memory_space=pl.ANY)),
            scratch_shapes=[
                pltpu.VMEM((n, n), F32),
                pltpu.VMEM((n, n), BF16),
                pltpu.VMEM((n, n), BF16),
                pltpu.VMEM((chunks, 2 * ny, rb, ch), F32),
                pltpu.VMEM((chunks, ncol, rb, ch), F32),
                pltpu.VMEM((chunks, n, ch), BF16),
                pltpu.VMEM((chunks, n, ch), BF16),
                pltpu.VMEM((chunks, n, ch), F32),
                pltpu.VMEM((chunks, n // 2, ch), F32),
                pltpu.VMEM((chunks, xln * ny - 1, rb, ch), F32),
                pltpu.VMEM((w, rb), BF16),
                pltpu.VMEM((w, rb), BF16),
                pltpu.VMEM((chunks, w, ch), F32),
                pltpu.VMEM((chunks, d_half, ch), F32),
                pltpu.VMEM((chunks, ny - 1, d_a, ch), F32),
                pltpu.VMEM((chunks, nx - 1, d_rows, ch), F32),
                pltpu.VMEM((chunks, nz, d_rows, ch), F32),
                pltpu.VMEM((chunks, w, ch), F32),
                pltpu.VMEM((chunks, d_rows, ch), F32),
                dma((1 + chunks,)),
                dma((chunks, ncol)),
                dma((chunks, 2 * ny)),
                dma,
                dma,
                dma((2,)),
            ]
            + [dma, dma((chunks,))] * 9
            + [dma((chunks,))],
            compiler_params=pltpu.CompilerParams(
                collective_id=0, has_side_effects=True, vmem_limit_bytes=63 * 2**20
            ),
        )(inverse, pattern, factor, diag_inverse)
        return panel.transpose(1, 0, 2).reshape(rb, w), diag

    return body


def solution(mesh):
    return jax.shard_map(
        make(FULL),
        mesh=mesh,
        in_specs=(P("row", "col"), P(), P(("row", "col"), None), P()),
        out_specs=(P(("row", "col"), None), P()),
        check_vma=False,
    )
```
